512 devices in a mesh: expert: 64 (over y_hi, z, core), hid: 8 (over y_lo, x).
Axes of the slice: x: 4, y: 8 (y_hi: 4, y_lo: 2; y = y_hi * 2 + y_lo), z: 8, core: 2. Of those that a mesh axis runs over, the one named last changes fastest.
Arguments:
- tokens: bfloat16 [16384, 2048], P('expert', 'hid'), may hold values from -6 to 6
- out_grad: bfloat16 [16384, 2048], P('expert', 'hid'), may hold values from -6 to 6
- experts_of: int32 [16384, 2], P('expert'), may hold values from 0 to 63, all different within a row; in each aligned block of 256 rows (0 to 255, 256 to 511, ...) at most 16 rows name the same one
- gates: float32 [16384, 2], P('expert'), may hold values from 0.1 to 1
- place_before: int32 [64], replicated, may hold values from 0 to 63, each once
- partner: int32 [64], replicated, may hold values from 0 to 63, as said below
- w_in: bfloat16 [64, 1152, 2048], P('expert', 'hid'), may hold values from -0.125 to 0.125
- w_out: bfloat16 [64, 1152, 2048], P('expert', 'hid'), may hold values from -0.1875 to 0.1875
- m_in: bfloat16 [64, 1152, 2048], P('expert', 'hid'), may hold values from -24 to 24
- v_in: bfloat16 [64, 1152, 2048], P('expert', 'hid'), may hold values from 1 to 100
Outputs:
- mixed: bfloat16 [16384, 2048], P('expert', 'hid')
- input_grad: bfloat16 [16384, 2048], P('expert', 'hid')
- gate_grad: float32 [16384, 2], P('expert')
- new_w_in: bfloat16 [64, 1152, 2048], P('expert', 'hid')
- new_m_in: bfloat16 [64, 1152, 2048], P('expert', 'hid')
- new_v_in: bfloat16 [64, 1152, 2048], P('expert', 'hid')
The draws below stay inside these ranges and needn't reach their ends.
Inputs may be any that keep to these rules, and one draw needn't show every extreme that they name: `experts_of`: each row names 2 different experts; in each aligned block of 256 rows (the rows of one index of expert) no expert is named by more than 16 rows. `place_before`: a permutation of the experts. An involution: for one bit b common to all slots, partner[j] is j or j XOR 2^b, and slot 0 always takes the other.
All inputs are finite; a program needn't handle non-finite values.
Results may differ from the reference program's by a relative error of at most 0.02.
Values may be sent and summed in bfloat16 or wider, within the bound.
No kernel may reach another device: no remote copies, remote signals or barrier semaphores. Data moves between devices by JAX's collectives and lax.ppermute only.
A program may use at most 128 MiB of HBM per device.

```python
import math
import jax
import jax.numpy as jnp
import numpy as np
from jax import lax

D = 2048
H = 1152
TOP = 2
TOK_DEV = 256
EXPERTS = 64
CAP = 16
TOKENS = 16384
N_EXPERT = 64
N_HID = 8


def draw_partner(key, part):
    key = jax.random.fold_in(key, 7)
    levels = N_EXPERT.bit_length() - 1
    first_key, second_key = jax.random.split(key)
    chosen_bit = jax.random.randint(first_key, (), 0, levels)
    slots = jnp.arange(N_EXPERT, dtype=jnp.int32)
    mates = jnp.bitwise_xor(slots, jnp.left_shift(jnp.int32(1), chosen_bit.astype(jnp.int32)))
    lowest = jnp.minimum(slots, mates)
    flags = jax.random.randint(second_key, (N_EXPERT,), 0, 2)
    moving = jnp.logical_or(flags[lowest] == 1, lowest == 0)
    return jnp.where(moving, mates, slots).astype(jnp.int32)


def steps_of(own_key, extent, cuts, low, high):
    loudness, own = 1.0, jax.random.fold_in(own_key, 6)
    for position, shards_of in cuts:
        steps = jnp.exp(jax.random.uniform(jax.random.fold_in(own, position), (shards_of,), jnp.float32, low / len(cuts), high / len(cuts)))
        loudness = loudness * jnp.repeat(steps, extent[position] // shards_of).reshape([-1 if axis == position else 1 for axis in range(len(extent))])
    return loudness


def routed_block(key, own, number, rows, number_of, top, most, lean):
    sequence = jax.random.permutation(key, number_of)
    crowded, ordinary = shares(number_of, rows * top, most, lean, True), shares(number_of, rows * top, most, lean, False)
    places = jnp.arange(number_of)

    def named(tallies, offset_by):
        used = int((tallies > 0).sum())
        fixed = max(1, used // 4)
        passed = fixed + (places - fixed + offset_by * (used - fixed)) % max(1, number_of - fixed)
        return jnp.zeros((number_of,), jnp.int32).at[sequence[jnp.where(places < fixed, places, passed)]].set(jnp.asarray(tallies, jnp.int32))

    tallies = jnp.where(number % 4 == 0, named(crowded, number // 4), named(ordinary, number - number // 4 - 1))
    mixed = jax.random.permutation(jax.random.fold_in(own, 3), number_of)
    source_of, taker = mixed[0:number_of // 2 * 2:2], mixed[1:number_of // 2 * 2:2]
    margin = jnp.minimum(tallies[source_of] - 1, most - tallies[taker]) // 2
    margin = jnp.where((source_of == sequence[0]) | (taker == sequence[0]) | (tallies[taker] == 0), 0, jnp.maximum(margin, 0))
    passed = jax.random.randint(jax.random.fold_in(own, 4), (number_of // 2,), 0, 1 << 20) % (margin + 1)
    tallies = tallies.at[source_of].add(-passed).at[taker].add(passed)
    items = jnp.searchsorted(jnp.cumsum(tallies), jnp.arange(rows * top), side="right").astype(jnp.int32)
    listing = items.reshape(top, rows).T
    listing = listing[jax.random.permutation(jax.random.fold_in(own, 1), rows)]
    offset_by = jax.random.randint(jax.random.fold_in(own, 2), (rows, 1), 0, top)
    return jnp.take_along_axis(listing, (jnp.arange(top)[None, :] + offset_by) % top, axis=1)


def shares(amount, total, bound, lean, full):
    loads = [(1 << 20) // math.isqrt(grade ** lean) + 1 for grade in range(1, amount + 1)]
    largest = bound if full else min(bound, max(-(-total // amount), total * loads[0] // sum(loads)))
    least = 1 if total - largest >= amount - 1 else 0
    holding, surplus = [largest] + [least] * (amount - 1), total - largest - least * (amount - 1)
    while surplus > 0:
        free = [i for i in range(1, amount) if holding[i] < largest] or [i for i in range(1, amount) if holding[i] < bound]
        pool, left = sum([loads[i] for i in free]), surplus
        for i in free:
            more = min(bound - holding[i], max(1, left * loads[i] // pool), surplus)
            holding[i] = holding[i] + more
            surplus = surplus - more
    return np.array(holding)


def noise(key, dims, deviation, most, shards=(), kind=jnp.bfloat16):
    values = jax.random.normal(key, dims, jnp.float32) * deviation
    if len(shards) > 0:
        values = steps_of(key, dims, shards, -0.22, 0.18) * values
    return jnp.clip(values, min=-most, max=most).astype(kind)


def setup_inputs(seed: int = 0) -> dict:
    key_list = jax.random.split(jax.random.key(seed), 11)
    tokens = noise(key_list[0], (TOKENS, D), 1.0, 6.0, ((0, 64), (1, 8)))
    out_grad = noise(key_list[1], (TOKENS, D), 1.0, 6.0, ((0, 64), (1, 8)))
    experts_of_keys = jax.random.split(jax.random.fold_in(key_list[2], 1), TOKENS // TOK_DEV)
    experts_of_turns = jax.random.permutation(jax.random.fold_in(key_list[2], 3), TOKENS // TOK_DEV)
    experts_of = jax.vmap(lambda own, number: routed_block(jax.random.fold_in(key_list[2], 2), own, number, TOK_DEV, EXPERTS, TOP, CAP, 2))(experts_of_keys, experts_of_turns).reshape((TOKENS, TOP))
    gates = jnp.clip(0.1 + 0.9 * jax.random.uniform(key_list[3], (TOKENS, TOP), jnp.float32) ** steps_of(key_list[3], (TOKENS, TOP), ((0, 64),), -0.2, 0.2), 0.1, 1.0)
    place_before = jax.random.permutation(key_list[4], N_EXPERT).astype(jnp.int32)
    partner = draw_partner(jax.random.fold_in(key_list[10], 71), 0)
    w_in = noise(key_list[6], (N_EXPERT, H, D), D ** -0.5, 0.125, ((0, 64), (1, 8)))
    w_out = noise(key_list[7], (N_EXPERT, H, D), H ** -0.5, 0.1875, ((0, 64), (1, 8)))
    m_in = noise(key_list[8], (N_EXPERT, H, D), 4.0, 24.0, ((0, 64), (1, 8)))
    v_in = jnp.clip(jnp.exp(math.log(100.0) - 4.6051702 * jax.random.uniform(key_list[9], (N_EXPERT, H, D), jnp.float32) ** steps_of(key_list[9], (N_EXPERT, H, D), ((0, 64), (1, 8)), -0.2, 0.2)), 1.0, 100.0).astype(jnp.bfloat16)
    return {"tokens": tokens, "out_grad": out_grad, "experts_of": experts_of, "gates": gates, "place_before": place_before, "partner": partner, "w_in": w_in, "w_out": w_out, "m_in": m_in, "v_in": v_in}


beta_first = 0.9
beta_second = 0.95
learn_rate = 0.001
decay_rate = 0.1
adam_eps = 1e-08
bias_first = 1.0 - 0.9 ** 10
bias_second = 1.0 - 0.95 ** 10

def group_sum(left, right):
    rows = left.shape[0]
    parted = left.astype(jnp.float32).reshape(rows, N_HID, H // N_HID).transpose(1, 0, 2)
    blocks = right.astype(jnp.float32).reshape(N_HID, H // N_HID, D)
    parts = jnp.einsum('grh,ghd->grd', parted, blocks, precision=lax.Precision.HIGHEST)
    parts = lax.optimization_barrier(parts.astype(jnp.bfloat16))
    return lax.optimization_barrier(jnp.sum(parts.astype(jnp.float32), axis=0)).astype(jnp.bfloat16)

def adamw(weight, first, second, grads):
    first_new = beta_first * first.astype(jnp.float32) + (1.0 - beta_first) * grads
    second_new = beta_second * second.astype(jnp.float32) + (1.0 - beta_second) * grads * grads
    wide = weight.astype(jnp.float32)
    ratio = first_new / bias_first / (jnp.sqrt(second_new / bias_second) + adam_eps)
    wide = wide - learn_rate * (ratio + decay_rate * wide)
    return (wide.astype(jnp.bfloat16), first_new.astype(jnp.bfloat16), second_new.astype(jnp.bfloat16))

def expert_pass(packed):
    x_block, dy_block, wa, wb, ma, va = packed
    x_rows = x_block.reshape(-1, D)
    dy_rows = dy_block.reshape(-1, D)
    pre = jnp.dot(x_rows, wa.T, preferred_element_type=jnp.float32)
    act = jax.nn.silu(pre).astype(jnp.bfloat16)
    y_rows = group_sum(act, wb)
    dact = jnp.dot(dy_rows, wb.T, preferred_element_type=jnp.float32)
    sig = jax.nn.sigmoid(pre)
    dpre = (dact * sig * (1.0 + pre * (1.0 - sig))).astype(jnp.bfloat16)
    grad_in = jnp.dot(dpre.T, x_rows, preferred_element_type=jnp.float32)
    dx_rows = group_sum(dpre, wa)
    new_wa, new_ma, new_va = adamw(wa, ma, va, grad_in)
    return (y_rows.reshape(x_block.shape), dx_rows.reshape(x_block.shape), new_wa, new_ma, new_va)

def reference(tokens, out_grad, experts_of, gates, place_before, partner, w_in, w_out, m_in, v_in):
    slots = jnp.arange(N_EXPERT, dtype=jnp.int32)
    place_after = place_before[partner]
    owner = jnp.zeros((N_EXPERT,), jnp.int32).at[place_after].set(slots)
    pairs = TOK_DEV * TOP
    chosen = experts_of.reshape(N_EXPERT, pairs)
    onehot = (chosen[:, :, None] == slots[None, None, :]).astype(jnp.int32)
    rank = (lax.optimization_barrier(jnp.sum(jnp.cumsum(onehot, axis=1) * onehot, axis=2)) - 1).astype(jnp.int32)
    target = owner[chosen]
    source = jnp.broadcast_to(slots[:, None], chosen.shape)
    token_of = source * TOK_DEV + (jnp.arange(pairs, dtype=jnp.int32) // TOP)[None, :]
    x_pairs = tokens[token_of]
    dy_pairs = (gates.reshape(N_EXPERT, pairs)[:, :, None] * out_grad[token_of].astype(jnp.float32)).astype(jnp.bfloat16)
    x_all = jnp.zeros((N_EXPERT, N_EXPERT, CAP, D), jnp.bfloat16).at[target, source, rank].set(x_pairs)
    dy_all = jnp.zeros((N_EXPERT, N_EXPERT, CAP, D), jnp.bfloat16).at[target, source, rank].set(dy_pairs)
    results = lax.map(expert_pass, (x_all, dy_all, w_in[partner], w_out[partner], m_in[partner], v_in[partner]))
    y_all, dx_all, new_wa, new_ma, new_va = results
    y_slot = y_all[target, source, rank].reshape(TOKENS, TOP, D).astype(jnp.float32)
    dx_slot = dx_all[target, source, rank].reshape(TOKENS, TOP, D).astype(jnp.float32)
    mixed = lax.optimization_barrier(jnp.sum(gates[:, :, None] * y_slot, axis=1)).astype(jnp.bfloat16)
    gate_grad = lax.optimization_barrier(jnp.sum(out_grad.astype(jnp.float32)[:, None, :] * y_slot, axis=2))
    input_grad = lax.optimization_barrier(jnp.sum(dx_slot, axis=1)).astype(jnp.bfloat16)
    return (mixed, input_grad, gate_grad, new_wa, new_ma, new_va)
```

```python
from functools import partial

import jax
import jax.numpy as jnp
from jax import lax
from jax.sharding import PartitionSpec as P

beta_first = 0.9
beta_second = 0.95
learn_rate = 0.001
decay_rate = 0.1
adam_eps = 1e-08
bias_first = 1.0 - 0.9**10
bias_second = 1.0 - 0.95**10

ring = 4


def line_groups(hid_count):
    return [list(range(low, low + ring)) for low in range(0, hid_count, ring)]


def from_partner(value, bit):
    mask = 2**bit
    pairs = [(source, source ^ mask) for source in range(lax.axis_size("expert"))]
    return lax.ppermute(value, "expert", pairs)


def from_twin(value):
    pairs = [(source, source ^ ring) for source in range(lax.axis_size("hid"))]
    return lax.ppermute(value, "hid", pairs)


def swap_line(value):
    return lax.all_to_all(
        value,
        "hid",
        split_axis=0,
        concat_axis=0,
        tiled=True,
        axis_index_groups=line_groups(lax.axis_size("hid")),
    )


def gather_line(value):
    return swap_line(jnp.broadcast_to(value[None], (ring,) + value.shape))


def swap_slots(value):
    return lax.all_to_all(value, "expert", split_axis=0, concat_axis=0, tiled=True)


def adamw(weight, first, second, grads):
    first_new = beta_first * first.astype(jnp.float32) + (1.0 - beta_first) * grads
    second_new = beta_second * second.astype(jnp.float32) + (1.0 - beta_second) * grads * grads
    wide = weight.astype(jnp.float32)
    ratio = first_new / bias_first / (jnp.sqrt(second_new / bias_second) + adam_eps)
    wide = wide - learn_rate * (ratio + decay_rate * wide)
    return (
        wide.astype(jnp.bfloat16),
        first_new.astype(jnp.bfloat16),
        second_new.astype(jnp.bfloat16),
    )


def layer(
    bit, tokens, out_grad, experts_of, gates, place_before, staying, w_in, w_out, m_in, v_in
):
    slot_count = lax.axis_size("expert")
    hid_index = lax.axis_index("hid")
    line_index = hid_index % ring
    upper = hid_index >= ring
    slots = jnp.arange(slot_count, dtype=jnp.int32)
    tok_rows, feat_dev = tokens.shape
    top_count = experts_of.shape[1]
    pairs = tok_rows * top_count
    capacity = 2 * pairs // slot_count
    share = capacity // ring
    cells = slot_count * share
    half = ring * feat_dev

    token_grads = gather_line(jnp.concatenate([tokens, out_grad], axis=0))
    token_grads = jnp.concatenate([token_grads[i] for i in range(ring)], axis=1)
    tok_line, grad_line = token_grads[:tok_rows], token_grads[tok_rows:]

    wa_full = gather_line(w_in).reshape(-1, w_in.shape[1])
    wb_full = gather_line(w_out).reshape(-1, w_in.shape[1])
    w_moved, m_moved, v_moved = [from_partner(part, bit) for part in (w_in, m_in, v_in)]

    chosen = experts_of.reshape(-1)
    onehot = (chosen[:, None] == slots[None, :]).astype(jnp.int32)
    rank = jnp.sum(jnp.cumsum(onehot, axis=0) * onehot, axis=1) - 1
    owner = jnp.sum(
        jnp.where(place_before[None, :] == slots[:, None], slots[None, :], 0), axis=1
    )
    target = jnp.sum(onehot * owner[None, :], axis=1)
    cell = jnp.where(rank // share == line_index, target * share + rank % share, -1)
    pair_hit = cell[:, None] == jnp.arange(cells, dtype=jnp.int32)[None, :]
    gate_cell = jnp.sum(jnp.where(pair_hit, gates.reshape(-1)[:, None], 0.0), axis=0)
    pair_hit = pair_hit.astype(jnp.bfloat16)
    picker = jnp.sum(pair_hit.reshape(tok_rows, top_count, cells), axis=1)

    x_send = jnp.dot(picker.T, tok_line, preferred_element_type=jnp.float32)
    dy_send = jnp.dot(picker.T, grad_line, preferred_element_type=jnp.float32)
    dy_send = gate_cell[:, None] * dy_send
    sent = jnp.concatenate([x_send, dy_send], axis=1).astype(jnp.bfloat16)
    here = swap_slots(sent.reshape(slot_count, share, 2 * half)).reshape(cells, 2 * half)

    def both_halves(own):
        other = from_twin(own)
        return jnp.where(
            upper,
            jnp.concatenate([other, own], axis=1),
            jnp.concatenate([own, other], axis=1),
        )

    x_rows = both_halves(here[:, :half])
    dy_rows = both_halves(here[:, half:])

    pre = lax.dot_general(
        x_rows, wa_full, (((1,), (1,)), ((), ())), preferred_element_type=jnp.float32
    )
    act = jax.nn.silu(pre).astype(jnp.bfloat16)
    sig = jax.nn.sigmoid(pre)
    dact = lax.dot_general(
        dy_rows, wb_full, (((1,), (1,)), ((), ())), preferred_element_type=jnp.float32
    )
    dpre = (dact * sig * (1.0 + pre * (1.0 - sig))).astype(jnp.bfloat16)

    def own_half(part):
        part = part.astype(jnp.bfloat16)
        low, high = part[:, :half], part[:, half:]
        arrived = from_twin(jnp.where(upper, low, high))
        own = jnp.where(upper, high, low)
        return (own.astype(jnp.float32) + arrived.astype(jnp.float32)).astype(jnp.bfloat16)

    y_rows = own_half(jnp.dot(act, wb_full, preferred_element_type=jnp.float32))
    dx_rows = own_half(jnp.dot(dpre, wa_full, preferred_element_type=jnp.float32))
    grad_part = jnp.dot(dpre.T, x_rows, preferred_element_type=jnp.float32).astype(jnp.bfloat16)

    grads = swap_line(grad_part.reshape((ring,) + w_in.shape))
    grads = jnp.sum(grads.astype(jnp.float32), axis=0).astype(jnp.bfloat16)

    back = jnp.concatenate([y_rows, dx_rows], axis=1).reshape(slot_count, share, 2 * half)
    back = swap_slots(back).reshape(cells, 2 * half)
    y_back, dx_back = back[:, :half], back[:, half:]
    y_slot = jnp.dot(pair_hit, y_back, preferred_element_type=jnp.float32)
    y_slot = y_slot.reshape(tok_rows, top_count, half)
    mixed = jnp.sum(gates[:, :, None] * y_slot, axis=1).astype(jnp.bfloat16)
    gate_part = jnp.sum(grad_line.astype(jnp.float32)[:, None, :] * y_slot, axis=2)
    hid_count = lax.axis_size("hid")
    gate_grad = jnp.sum(
        lax.all_to_all(
            jnp.broadcast_to(gate_part.T[None], (hid_count, top_count, tok_rows)),
            "hid",
            split_axis=0,
            concat_axis=0,
            tiled=True,
        ),
        axis=0,
    ).T
    input_grad = jnp.dot(picker, dx_back, preferred_element_type=jnp.float32).astype(jnp.bfloat16)
    done = jnp.stack(
        [
            jnp.concatenate(
                [part[:, i * feat_dev : (i + 1) * feat_dev] for part in (mixed, input_grad)],
                axis=0,
            )
            for i in range(ring)
        ]
    )
    done = jnp.sum(swap_line(done).astype(jnp.float32), axis=0).astype(jnp.bfloat16)

    grads_moved = from_partner(grads, bit)
    new_w, new_m, new_v = adamw(
        jnp.where(staying, w_in, w_moved),
        jnp.where(staying, m_in, m_moved),
        jnp.where(staying, v_in, v_moved),
        jnp.where(staying, grads, grads_moved).astype(jnp.float32),
    )
    return done[:tok_rows], done[tok_rows:], gate_grad, new_w, new_m, new_v


def on_device(tokens, out_grad, experts_of, gates, place_before, partner, w_in, w_out, m_in, v_in):
    slot_count = lax.axis_size("expert")
    own_slot = lax.axis_index("expert")
    levels = slot_count.bit_length() - 1
    slots = jnp.arange(slot_count, dtype=jnp.int32)
    largest = jnp.max(jnp.bitwise_xor(partner, slots))
    bit_range = jnp.arange(levels, dtype=jnp.int32)
    chosen_bit = jnp.sum(
        jnp.where(largest == jnp.left_shift(jnp.int32(1), bit_range), bit_range, 0)
    )
    staying = jnp.sum(jnp.where(slots == own_slot, partner, 0)) == own_slot
    mixed, input_grad, gate_grad, new_w, new_m, new_v = lax.switch(
        chosen_bit,
        [partial(layer, bit) for bit in range(levels)],
        tokens,
        out_grad,
        experts_of,
        gates,
        place_before,
        staying,
        w_in[0],
        w_out[0],
        m_in[0],
        v_in[0],
    )
    return (mixed, input_grad, gate_grad, new_w[None], new_m[None], new_v[None])


def solution(mesh):
    return jax.shard_map(
        on_device,
        mesh=mesh,
        in_specs=(
            P("expert", "hid"),
            P("expert", "hid"),
            P("expert", None),
            P("expert", None),
            P(),
            P(),
            P("expert", "hid", None),
            P("expert", "hid", None),
            P("expert", "hid", None),
            P("expert", "hid", None),
        ),
        out_specs=(
            P("expert", "hid"),
            P("expert", "hid"),
            P("expert", None),
            P("expert", "hid", None),
            P("expert", "hid", None),
            P("expert", "hid", None),
        ),
        check_vma=False,
    )
```

```python
import jax
import jax.numpy as jnp
from jax import lax
from jax.sharding import PartitionSpec as P

beta_first = 0.9
beta_second = 0.95
learn_rate = 0.001
decay_rate = 0.1
adam_eps = 1e-08
bias_first = 1.0 - 0.9**10
bias_second = 1.0 - 0.95**10

ring = 4


def line_groups(hid_count):
    return [list(range(low, low + ring)) for low in range(0, hid_count, ring)]


def from_partner(value, bit):
    mask = 2**bit
    pairs = [(source, source ^ mask) for source in range(lax.axis_size("expert"))]
    return lax.ppermute(value, "expert", pairs)


def from_twin(value):
    pairs = [(source, source ^ ring) for source in range(lax.axis_size("hid"))]
    return lax.ppermute(value, "hid", pairs)


def swap_line(value):
    return lax.all_to_all(
        value,
        "hid",
        split_axis=0,
        concat_axis=0,
        tiled=True,
        axis_index_groups=line_groups(lax.axis_size("hid")),
    )


def gather_line(value):
    return swap_line(jnp.broadcast_to(value[None], (ring,) + value.shape))


def swap_slots(value):
    return lax.all_to_all(value, "expert", split_axis=0, concat_axis=0, tiled=True)


def adamw(weight, first, second, grads):
    first_new = beta_first * first.astype(jnp.float32) + (1.0 - beta_first) * grads
    second_new = beta_second * second.astype(jnp.float32) + (1.0 - beta_second) * grads * grads
    wide = weight.astype(jnp.float32)
    ratio = first_new / bias_first / (jnp.sqrt(second_new / bias_second) + adam_eps)
    wide = wide - learn_rate * (ratio + decay_rate * wide)
    return (
        wide.astype(jnp.bfloat16),
        first_new.astype(jnp.bfloat16),
        second_new.astype(jnp.bfloat16),
    )


def on_device(tokens, out_grad, experts_of, gates, place_before, partner, w_in, w_out, m_in, v_in):
    w_in, w_out, m_in, v_in = w_in[0], w_out[0], m_in[0], v_in[0]
    slot_count = lax.axis_size("expert")
    hid_count = lax.axis_size("hid")
    own_slot = lax.axis_index("expert")
    line_index = lax.axis_index("hid") % ring
    upper = lax.axis_index("hid") >= ring
    levels = slot_count.bit_length() - 1
    slots = jnp.arange(slot_count, dtype=jnp.int32)
    tok_rows, feat_dev = tokens.shape
    top_count = experts_of.shape[1]
    pairs = tok_rows * top_count
    capacity = 2 * pairs // slot_count
    share = capacity // ring
    cells = slot_count * share
    half = ring * feat_dev

    largest = jnp.max(jnp.bitwise_xor(partner, slots))
    bit_range = jnp.arange(levels, dtype=jnp.int32)
    chosen_bit = jnp.sum(
        jnp.where(largest == jnp.left_shift(jnp.int32(1), bit_range), bit_range, 0)
    )
    staying = jnp.sum(jnp.where(slots == own_slot, partner, 0)) == own_slot

    def move(parts):
        branches = [
            lambda parts, bit=bit: [from_partner(part, bit) for part in parts]
            for bit in range(levels)
        ]
        return lax.switch(chosen_bit, branches, parts)

    token_grads = gather_line(jnp.concatenate([tokens, out_grad], axis=0))
    token_grads = jnp.concatenate([token_grads[i] for i in range(ring)], axis=1)
    tok_line, grad_line = token_grads[:tok_rows], token_grads[tok_rows:]

    weights = lax.all_gather(
        jnp.stack([w_in, w_out]),
        "hid",
        axis=1,
        tiled=True,
        axis_index_groups=line_groups(hid_count),
    )
    wa_full, wb_full = weights[0], weights[1]

    chosen = experts_of.reshape(-1)
    onehot = (chosen[:, None] == slots[None, :]).astype(jnp.int32)
    rank = jnp.sum(jnp.cumsum(onehot, axis=0) * onehot, axis=1) - 1
    owner = jnp.sum(
        jnp.where(place_before[None, :] == slots[:, None], slots[None, :], 0), axis=1
    )
    target = jnp.sum(onehot * owner[None, :], axis=1)
    cell = jnp.where(rank // share == line_index, target * share + rank % share, -1)
    pair_hit = cell[:, None] == jnp.arange(cells, dtype=jnp.int32)[None, :]
    gate_cell = jnp.sum(jnp.where(pair_hit, gates.reshape(-1)[:, None], 0.0), axis=0)
    picker = jnp.sum(
        pair_hit.astype(jnp.bfloat16).reshape(tok_rows, top_count, cells), axis=1
    )

    x_send = jnp.dot(picker.T, tok_line, preferred_element_type=jnp.float32)
    grad_cell = jnp.dot(picker.T, grad_line, preferred_element_type=jnp.float32)
    sent = jnp.concatenate([x_send, gate_cell[:, None] * grad_cell], axis=1).astype(jnp.bfloat16)
    sent = sent.reshape(slot_count, share, 2 * half)

    sent, m_in, v_in = lax.optimization_barrier((sent, m_in, v_in))
    here = swap_slots(sent)
    m_moved, v_moved = move([m_in, v_in])
    here, m_moved, v_moved = lax.optimization_barrier((here, m_moved, v_moved))
    here = here.reshape(cells, 2 * half)

    def both_halves(own):
        other = from_twin(own)
        return jnp.where(
            upper,
            jnp.concatenate([other, own], axis=1),
            jnp.concatenate([own, other], axis=1),
        )

    x_rows = both_halves(here[:, :half])
    dy_rows = both_halves(here[:, half:])

    pre = lax.dot_general(
        x_rows, wa_full, (((1,), (1,)), ((), ())), preferred_element_type=jnp.float32
    )
    act = jax.nn.silu(pre).astype(jnp.bfloat16)
    sig = jax.nn.sigmoid(pre)
    dact = lax.dot_general(
        dy_rows, wb_full, (((1,), (1,)), ((), ())), preferred_element_type=jnp.float32
    )
    dpre = (dact * sig * (1.0 + pre * (1.0 - sig))).astype(jnp.bfloat16)

    def own_half(part):
        part = part.astype(jnp.bfloat16)
        low, high = part[:, :half], part[:, half:]
        arrived = from_twin(jnp.where(upper, low, high))
        own = jnp.where(upper, high, low)
        return (own.astype(jnp.float32) + arrived.astype(jnp.float32)).astype(jnp.bfloat16)

    y_rows = own_half(jnp.dot(act, wb_full, preferred_element_type=jnp.float32))
    dx_rows = own_half(jnp.dot(dpre, wa_full, preferred_element_type=jnp.float32))
    grad_part = jnp.dot(dpre.T, x_rows, preferred_element_type=jnp.float32).astype(jnp.bfloat16)
    grads = swap_line(grad_part.reshape((ring,) + w_in.shape))
    grads = jnp.sum(grads.astype(jnp.float32), axis=0).astype(jnp.bfloat16)

    back = jnp.concatenate([y_rows, dx_rows], axis=1).reshape(slot_count, share, 2 * half)
    back, grads, w_in = lax.optimization_barrier((back, grads, w_in))
    back = swap_slots(back)
    grads_moved, w_moved = move([grads, w_in])
    back, grads_moved, w_moved = lax.optimization_barrier((back, grads_moved, w_moved))
    back = back.reshape(cells, 2 * half)
    y_back, dx_back = back[:, :half], back[:, half:]
    y_wide = y_back.astype(jnp.float32)
    gate_cell_grad = jnp.sum(grad_cell * y_wide, axis=1)
    gate_part = jnp.sum(jnp.where(pair_hit, gate_cell_grad[None, :], 0.0), axis=1)
    gate_part = gate_part.reshape(tok_rows, top_count).T
    gate_part = gate_part + from_twin(gate_part)
    gate_terms = []
    for _ in range(3):
        term = gate_part.astype(jnp.bfloat16)
        gate_part = gate_part - term.astype(jnp.float32)
        gate_terms.append(term)
    y_wide = gate_cell[:, None] * y_wide
    y_high = y_wide.astype(jnp.bfloat16)
    y_low = (y_wide - y_high.astype(jnp.float32)).astype(jnp.bfloat16)
    mixed = jnp.dot(
        jnp.concatenate([picker, picker], axis=1),
        jnp.concatenate([y_high, y_low], axis=0),
        preferred_element_type=jnp.float32,
    ).astype(jnp.bfloat16)
    input_grad = jnp.dot(picker, dx_back, preferred_element_type=jnp.float32).astype(jnp.bfloat16)
    spare = jnp.zeros((16 - 3 * top_count, tok_rows), jnp.bfloat16)
    extra = jnp.concatenate(gate_terms + [spare], axis=0)
    done = jnp.stack(
        [
            jnp.concatenate(
                [part[:, i * feat_dev : (i + 1) * feat_dev] for part in (mixed, input_grad)]
                + [extra],
                axis=0,
            )
            for i in range(ring)
        ]
    )
    done = jnp.sum(swap_line(done).astype(jnp.float32), axis=0)
    gate_terms = done[2 * tok_rows : 2 * tok_rows + 3 * top_count]
    gate_grad = jnp.sum(gate_terms.reshape(3, top_count, tok_rows), axis=0).T
    done = done[: 2 * tok_rows].astype(jnp.bfloat16)

    new_w, new_m, new_v = adamw(
        jnp.where(staying, w_in, w_moved),
        jnp.where(staying, m_in, m_moved),
        jnp.where(staying, v_in, v_moved),
        jnp.where(staying, grads, grads_moved).astype(jnp.float32),
    )
    return (
        done[:tok_rows],
        done[tok_rows:],
        gate_grad,
        new_w[None],
        new_m[None],
        new_v[None],
    )


def solution(mesh):
    return jax.shard_map(
        on_device,
        mesh=mesh,
        in_specs=(
            P("expert", "hid"),
            P("expert", "hid"),
            P("expert", None),
            P("expert", None),
            P(),
            P(),
            P("expert", "hid", None),
            P("expert", "hid", None),
            P("expert", "hid", None),
            P("expert", "hid", None),
        ),
        out_specs=(
            P("expert", "hid"),
            P("expert", "hid"),
            P("expert", None),
            P("expert", "hid", None),
            P("expert", "hid", None),
            P("expert", "hid", None),
        ),
        check_vma=False,
    )
```

```python
import jax
import jax.numpy as jnp
from jax import lax
from jax.sharding import PartitionSpec as P

beta_first = 0.9
beta_second = 0.95
learn_rate = 0.001
decay_rate = 0.1
adam_eps = 1e-08
bias_first = 1.0 - 0.9**10
bias_second = 1.0 - 0.95**10

ring = 4


def line_groups(hid_count):
    return [list(range(low, low + ring)) for low in range(0, hid_count, ring)]


def from_partner(value, bit):
    mask = 2**bit
    pairs = [(source, source ^ mask) for source in range(lax.axis_size("expert"))]
    return lax.ppermute(value, "expert", pairs)


def along_line(value, step):
    pairs = [
        (source, source // ring * ring + (source + step) % ring)
        for source in range(lax.axis_size("hid"))
    ]
    return lax.ppermute(value, "hid", pairs)


def swap(value, axis):
    return lax.all_to_all(value, axis, split_axis=0, concat_axis=0, tiled=True)


def adamw(weight, first, second, grads):
    first_new = beta_first * first.astype(jnp.float32) + (1.0 - beta_first) * grads
    second_new = beta_second * second.astype(jnp.float32) + (1.0 - beta_second) * grads * grads
    wide = weight.astype(jnp.float32)
    ratio = first_new / bias_first / (jnp.sqrt(second_new / bias_second) + adam_eps)
    wide = wide - learn_rate * (ratio + decay_rate * wide)
    return (
        wide.astype(jnp.bfloat16),
        first_new.astype(jnp.bfloat16),
        second_new.astype(jnp.bfloat16),
    )


def on_device(tokens, out_grad, experts_of, gates, place_before, partner, w_in, w_out, m_in, v_in):
    w_in, w_out, m_in, v_in = w_in[0], w_out[0], m_in[0], v_in[0]
    slot_count = lax.axis_size("expert")
    hid_count = lax.axis_size("hid")
    own_slot = lax.axis_index("expert")
    line_index = lax.axis_index("hid") % ring
    levels = slot_count.bit_length() - 1
    slots = jnp.arange(slot_count, dtype=jnp.int32)
    tok_rows, feat_dev = tokens.shape
    top_count = experts_of.shape[1]
    pairs = tok_rows * top_count
    capacity = 2 * pairs // slot_count
    cells = slot_count * capacity
    rows = cells // ring
    twins = hid_count // ring

    largest = jnp.max(jnp.bitwise_xor(partner, slots))
    bit_range = jnp.arange(levels, dtype=jnp.int32)
    chosen_bit = jnp.sum(
        jnp.where(largest == jnp.left_shift(jnp.int32(1), bit_range), bit_range, 0)
    )
    staying = jnp.sum(jnp.where(slots == own_slot, partner, 0)) == own_slot

    def move(parts):
        branches = [
            lambda parts, bit=bit: [from_partner(part, bit) for part in parts]
            for bit in range(levels)
        ]
        return lax.switch(chosen_bit, branches, parts)

    stacked, experts_of, tokens, out_grad = lax.optimization_barrier(
        (jnp.stack([w_in, w_out]), experts_of, tokens, out_grad)
    )
    weights = lax.all_gather(
        stacked, "hid", axis=1, tiled=True, axis_index_groups=line_groups(hid_count)
    )

    chosen = experts_of.reshape(-1)
    onehot = (chosen[:, None] == slots[None, :]).astype(jnp.int32)
    rank = jnp.sum(jnp.cumsum(onehot, axis=0) * onehot, axis=1) - 1
    owner = jnp.sum(
        jnp.where(place_before[None, :] == slots[:, None], slots[None, :], 0), axis=1
    )
    target = jnp.sum(onehot * owner[None, :], axis=1)
    cell = target * capacity + rank
    pair_hit = cell[:, None] == jnp.arange(cells, dtype=jnp.int32)[None, :]
    gate_cell = jnp.sum(jnp.where(pair_hit, gates.reshape(-1)[:, None], 0.0), axis=0)
    picker = jnp.sum(
        pair_hit.astype(jnp.bfloat16).reshape(tok_rows, top_count, cells), axis=1
    )

    x_send = jnp.dot(picker.T, tokens, preferred_element_type=jnp.float32)
    grad_cell = jnp.dot(picker.T, out_grad, preferred_element_type=jnp.float32)
    dy_send = gate_cell[:, None] * grad_cell
    sent = jnp.concatenate(
        [
            part.astype(jnp.bfloat16).reshape(slot_count, capacity, feat_dev)
            for part in (x_send, dy_send)
        ],
        axis=1,
    )
    here = swap(sent, "expert")
    here = jnp.broadcast_to(
        here.reshape(1, ring, 2 * rows, feat_dev), (twins, ring, 2 * rows, feat_dev)
    ).reshape(hid_count, 2 * rows, feat_dev)
    here, weights = lax.optimization_barrier((here, weights))
    wa_full, wb_full = weights[0], weights[1]
    here = swap(here, "hid")
    here = here.reshape(hid_count, slot_count // ring, 2, capacity, feat_dev)
    x_rows, dy_rows = [
        jnp.concatenate(
            [here[i, :, kind].reshape(rows, feat_dev) for i in range(hid_count)], axis=1
        )
        for kind in range(2)
    ]

    pre = lax.dot_general(
        x_rows, wa_full, (((1,), (1,)), ((), ())), preferred_element_type=jnp.float32
    )
    act = jax.nn.silu(pre).astype(jnp.bfloat16)
    sig = jax.nn.sigmoid(pre)
    dact = lax.dot_general(
        dy_rows, wb_full, (((1,), (1,)), ((), ())), preferred_element_type=jnp.float32
    )
    dpre = (dact * sig * (1.0 + pre * (1.0 - sig))).astype(jnp.bfloat16)

    y_part = jnp.dot(act, wb_full, preferred_element_type=jnp.float32).astype(jnp.bfloat16)
    dx_part = jnp.dot(dpre, wa_full, preferred_element_type=jnp.float32).astype(jnp.bfloat16)
    back = jnp.concatenate(
        [
            part.reshape(slot_count // ring, 1, capacity, hid_count * feat_dev)
            for part in (y_part, dx_part)
        ],
        axis=1,
    )
    back = jnp.transpose(back.reshape(2 * rows, hid_count, feat_dev), (1, 0, 2))
    back, dpre = lax.optimization_barrier((back, dpre))
    back = swap(back, "hid")
    grad_part = jnp.dot(dpre.T, x_rows, preferred_element_type=jnp.float32).astype(jnp.bfloat16)
    grad_part = grad_part.reshape((ring,) + w_in.shape)
    grad_parts = [grad_part[(line_index + step) % ring] for step in range(ring)]
    back, grad_parts = lax.optimization_barrier((back, grad_parts))
    back = jnp.sum(
        back.reshape(twins, slot_count, 2 * capacity, feat_dev).astype(jnp.float32), axis=0
    ).astype(jnp.bfloat16)

    back, grad_parts = lax.optimization_barrier((back, grad_parts))
    back = swap(back, "expert")
    grads = grad_parts[0].astype(jnp.float32)
    for step in (1, 3, 2):
        grads = grads + along_line(grad_parts[step], step).astype(jnp.float32)
    states = adamw(w_in, m_in, v_in, grads)
    y_back, dx_back = back[:, :capacity], back[:, capacity:]
    y_wide = y_back.reshape(cells, feat_dev).astype(jnp.float32)
    gate_cell_grad = jnp.sum(grad_cell * y_wide, axis=1)
    gate_part = jnp.sum(jnp.where(pair_hit, gate_cell_grad[None, :], 0.0), axis=1)
    gate_part = gate_part.reshape(tok_rows, top_count).T
    gate_part = jnp.broadcast_to(gate_part[None], (hid_count, top_count, tok_rows))
    gate_part, states = lax.optimization_barrier((gate_part, states))
    gate_part = swap(gate_part, "hid")
    moved = move(states)
    gate_part, moved = lax.optimization_barrier((gate_part, moved))
    gate_grad = jnp.sum(gate_part, axis=0).T

    y_wide = gate_cell[:, None] * y_wide
    y_high = y_wide.astype(jnp.bfloat16)
    y_low = (y_wide - y_high.astype(jnp.float32)).astype(jnp.bfloat16)
    mixed = jnp.dot(
        jnp.concatenate([picker, picker], axis=1),
        jnp.concatenate([y_high, y_low], axis=0),
        preferred_element_type=jnp.float32,
    ).astype(jnp.bfloat16)
    input_grad = jnp.dot(
        picker, dx_back.reshape(cells, feat_dev), preferred_element_type=jnp.float32
    ).astype(jnp.bfloat16)

    states = [jnp.where(staying, own, other)[None] for own, other in zip(states, moved)]
    return mixed, input_grad, gate_grad, *states


def solution(mesh):
    return jax.shard_map(
        on_device,
        mesh=mesh,
        in_specs=(
            P("expert", "hid"),
            P("expert", "hid"),
            P("expert", None),
            P("expert", None),
            P(),
            P(),
            P("expert", "hid", None),
            P("expert", "hid", None),
            P("expert", "hid", None),
            P("expert", "hid", None),
        ),
        out_specs=(
            P("expert", "hid"),
            P("expert", "hid"),
            P("expert", None),
            P("expert", "hid", None),
            P("expert", "hid", None),
            P("expert", "hid", None),
        ),
        check_vma=False,
    )
```

```python
import jax
import jax.numpy as jnp
from jax import lax
from jax.sharding import PartitionSpec as P

beta_first = 0.9
beta_second = 0.95
learn_rate = 0.001
decay_rate = 0.1
adam_eps = 1e-08
bias_first = 1.0 - 0.9**10
bias_second = 1.0 - 0.95**10

ring = 4


def line_groups(hid_count):
    return [list(range(low, low + ring)) for low in range(0, hid_count, ring)]


def from_partner(value, bit):
    mask = 2**bit
    pairs = [(source, source ^ mask) for source in range(lax.axis_size("expert"))]
    return lax.ppermute(value, "expert", pairs)


def along_line(value, step):
    pairs = [
        (source, source // ring * ring + (source + step) % ring)
        for source in range(lax.axis_size("hid"))
    ]
    return lax.ppermute(value, "hid", pairs)


def swap(value, axis):
    return lax.all_to_all(value, axis, split_axis=0, concat_axis=0, tiled=True)


def new_moments(first, second, grads):
    first_new = beta_first * first.astype(jnp.float32) + (1.0 - beta_first) * grads
    second_new = beta_second * second.astype(jnp.float32) + (1.0 - beta_second) * grads * grads
    return [first_new.astype(jnp.bfloat16), second_new.astype(jnp.bfloat16)]


def new_weight(weight, first_new, second_new):
    first_new, second_new = first_new.astype(jnp.float32), second_new.astype(jnp.float32)
    wide = weight.astype(jnp.float32)
    ratio = first_new / bias_first / (jnp.sqrt(second_new / bias_second) + adam_eps)
    return (wide - learn_rate * (ratio + decay_rate * wide)).astype(jnp.bfloat16)


def on_device(tokens, out_grad, experts_of, gates, place_before, partner, w_in, w_out, m_in, v_in):
    w_in, w_out, m_in, v_in = w_in[0], w_out[0], m_in[0], v_in[0]
    slot_count = lax.axis_size("expert")
    hid_count = lax.axis_size("hid")
    own_slot = lax.axis_index("expert")
    line_index = lax.axis_index("hid") % ring
    levels = slot_count.bit_length() - 1
    slots = jnp.arange(slot_count, dtype=jnp.int32)
    tok_rows, feat_dev = tokens.shape
    top_count = experts_of.shape[1]
    pairs = tok_rows * top_count
    capacity = 2 * pairs // slot_count
    cells = slot_count * capacity
    rows = cells // ring
    twins = hid_count // ring

    largest = jnp.max(jnp.bitwise_xor(partner, slots))
    bit_range = jnp.arange(levels, dtype=jnp.int32)
    chosen_bit = jnp.sum(
        jnp.where(largest == jnp.left_shift(jnp.int32(1), bit_range), bit_range, 0)
    )
    staying = jnp.sum(jnp.where(slots == own_slot, partner, 0)) == own_slot

    short_bits, long_bits = range(2), range(2, levels)

    def move(parts, arrived=None, bits=range(levels)):
        def branch(bit):
            if bit in bits:
                return lambda parts, arrived: [from_partner(part, bit) for part in parts]
            return lambda parts, arrived: arrived

        return lax.switch(
            chosen_bit, [branch(bit) for bit in range(levels)], parts, arrived or parts
        )

    stacked, experts_of, tokens, out_grad = lax.optimization_barrier(
        (jnp.stack([w_in, w_out]), experts_of, tokens, out_grad)
    )
    weights = lax.all_gather(
        stacked, "hid", axis=1, tiled=True, axis_index_groups=line_groups(hid_count)
    )

    chosen = experts_of.reshape(-1)
    onehot = (chosen[:, None] == slots[None, :]).astype(jnp.int32)
    rank = jnp.sum(jnp.cumsum(onehot, axis=0) * onehot, axis=1) - 1
    owner = jnp.sum(
        jnp.where(place_before[None, :] == slots[:, None], slots[None, :], 0), axis=1
    )
    target = jnp.sum(onehot * owner[None, :], axis=1)
    cell = target * capacity + rank
    pair_hit = cell[:, None] == jnp.arange(cells, dtype=jnp.int32)[None, :]
    gate_cell = jnp.sum(jnp.where(pair_hit, gates.reshape(-1)[:, None], 0.0), axis=0)
    picker = jnp.sum(
        pair_hit.astype(jnp.bfloat16).reshape(tok_rows, top_count, cells), axis=1
    )

    x_send = jnp.dot(picker.T, tokens, preferred_element_type=jnp.float32)
    grad_cell = jnp.dot(picker.T, out_grad, preferred_element_type=jnp.float32)
    dy_send = gate_cell[:, None] * grad_cell
    sent = jnp.concatenate(
        [
            part.astype(jnp.bfloat16).reshape(slot_count, capacity, feat_dev)
            for part in (x_send, dy_send)
        ],
        axis=1,
    )
    here = swap(sent, "expert")
    here = jnp.broadcast_to(
        here.reshape(1, ring, 2 * rows, feat_dev), (twins, ring, 2 * rows, feat_dev)
    ).reshape(hid_count, 2 * rows, feat_dev)
    here = swap(here, "hid")
    weights, w_in = lax.optimization_barrier((weights, w_in))
    wa_full, wb_full = weights[0], weights[1]
    w_moved = move([w_in], bits=short_bits)
    here, w_moved = lax.optimization_barrier((here, w_moved))
    here = here.reshape(hid_count, slot_count // ring, 2, capacity, feat_dev)
    x_rows, dy_rows = [
        jnp.concatenate(
            [here[i, :, kind].reshape(rows, feat_dev) for i in range(hid_count)], axis=1
        )
        for kind in range(2)
    ]

    pre = lax.dot_general(
        x_rows, wa_full, (((1,), (1,)), ((), ())), preferred_element_type=jnp.float32
    )
    act = jax.nn.silu(pre).astype(jnp.bfloat16)
    sig = jax.nn.sigmoid(pre)
    dact = lax.dot_general(
        dy_rows, wb_full, (((1,), (1,)), ((), ())), preferred_element_type=jnp.float32
    )
    dpre = (dact * sig * (1.0 + pre * (1.0 - sig))).astype(jnp.bfloat16)

    y_part = jnp.dot(act, wb_full, preferred_element_type=jnp.float32).astype(jnp.bfloat16)
    dx_part = jnp.dot(dpre, wa_full, preferred_element_type=jnp.float32).astype(jnp.bfloat16)
    back = jnp.concatenate(
        [
            part.reshape(slot_count // ring, 1, capacity, hid_count * feat_dev)
            for part in (y_part, dx_part)
        ],
        axis=1,
    )
    back = jnp.transpose(back.reshape(2 * rows, hid_count, feat_dev), (1, 0, 2))
    back, dpre = lax.optimization_barrier((back, dpre))
    back = swap(back, "hid")
    grad_part = jnp.dot(dpre.T, x_rows, preferred_element_type=jnp.float32).astype(jnp.bfloat16)
    grads = lax.psum_scatter(
        grad_part,
        "hid",
        scatter_dimension=0,
        tiled=True,
        axis_index_groups=line_groups(hid_count),
    )
    grad_part, w_in, w_moved = lax.optimization_barrier((grad_part, w_in, w_moved))
    (w_moved,) = move([w_in], w_moved, bits=long_bits)
    back, _, w_moved = lax.optimization_barrier((back, grad_part, w_moved))
    back = jnp.sum(
        back.reshape(twins, slot_count, 2 * capacity, feat_dev).astype(jnp.float32), axis=0
    ).astype(jnp.bfloat16)

    back = swap(back, "expert")
    grads = grads.astype(jnp.float32)
    states = new_moments(m_in, v_in, grads)
    moved = move(states)
    back, states, moved = lax.optimization_barrier((back, states, moved))
    y_back, dx_back = back[:, :capacity], back[:, capacity:]
    y_wide = y_back.reshape(cells, feat_dev).astype(jnp.float32)
    gate_cell_grad = jnp.sum(grad_cell * y_wide, axis=1)
    gate_part = jnp.sum(jnp.where(pair_hit, gate_cell_grad[None, :], 0.0), axis=1)
    gate_part = gate_part.reshape(tok_rows, top_count).T
    gate_part = jnp.broadcast_to(gate_part[None], (hid_count, top_count, tok_rows))
    gate_grad = jnp.sum(swap(gate_part, "hid"), axis=0).T

    y_wide = gate_cell[:, None] * y_wide
    y_high = y_wide.astype(jnp.bfloat16)
    y_low = (y_wide - y_high.astype(jnp.float32)).astype(jnp.bfloat16)
    mixed = jnp.dot(
        jnp.concatenate([picker, picker], axis=1),
        jnp.concatenate([y_high, y_low], axis=0),
        preferred_element_type=jnp.float32,
    ).astype(jnp.bfloat16)
    input_grad = jnp.dot(
        picker, dx_back.reshape(cells, feat_dev), preferred_element_type=jnp.float32
    ).astype(jnp.bfloat16)

    new_m, new_v = [jnp.where(staying, own, other) for own, other in zip(states, moved)]
    new_w = new_weight(jnp.where(staying, w_in, w_moved), new_m, new_v)
    return mixed, input_grad, gate_grad, new_w[None], new_m[None], new_v[None]


def solution(mesh):
    return jax.shard_map(
        on_device,
        mesh=mesh,
        in_specs=(
            P("expert", "hid"),
            P("expert", "hid"),
            P("expert", None),
            P("expert", None),
            P(),
            P(),
            P("expert", "hid", None),
            P("expert", "hid", None),
            P("expert", "hid", None),
            P("expert", "hid", None),
        ),
        out_specs=(
            P("expert", "hid"),
            P("expert", "hid"),
            P("expert", None),
            P("expert", "hid", None),
            P("expert", "hid", None),
            P("expert", "hid", None),
        ),
        check_vma=False,
    )
```

```python
import jax
import jax.numpy as jnp
from jax import lax
from jax.sharding import PartitionSpec as P

beta_first = 0.9
beta_second = 0.95
learn_rate = 0.001
decay_rate = 0.1
adam_eps = 1e-08
bias_first = 1.0 - 0.9**10
bias_second = 1.0 - 0.95**10

ring = 4


def line_groups(hid_count):
    return [list(range(low, low + ring)) for low in range(0, hid_count, ring)]


def from_partner(value, bit):
    mask = 2**bit
    pairs = [(source, source ^ mask) for source in range(lax.axis_size("expert"))]
    return lax.ppermute(value, "expert", pairs)


def along_line(value, step):
    pairs = [
        (source, source // ring * ring + (source + step) % ring)
        for source in range(lax.axis_size("hid"))
    ]
    return lax.ppermute(value, "hid", pairs)


def swap(value, axis):
    return lax.all_to_all(value, axis, split_axis=0, concat_axis=0, tiled=True)


def new_moments(first, second, grads):
    first_new = beta_first * first.astype(jnp.float32) + (1.0 - beta_first) * grads
    second_new = beta_second * second.astype(jnp.float32) + (1.0 - beta_second) * grads * grads
    return [first_new.astype(jnp.bfloat16), second_new.astype(jnp.bfloat16)]


def new_weight(weight, first_new, second_new):
    first_new, second_new = first_new.astype(jnp.float32), second_new.astype(jnp.float32)
    wide = weight.astype(jnp.float32)
    ratio = first_new / bias_first / (jnp.sqrt(second_new / bias_second) + adam_eps)
    return (wide - learn_rate * (ratio + decay_rate * wide)).astype(jnp.bfloat16)


def on_device(tokens, out_grad, experts_of, gates, place_before, partner, w_in, w_out, m_in, v_in):
    w_in, w_out, m_in, v_in = w_in[0], w_out[0], m_in[0], v_in[0]
    slot_count = lax.axis_size("expert")
    hid_count = lax.axis_size("hid")
    own_slot = lax.axis_index("expert")
    line_index = lax.axis_index("hid") % ring
    levels = slot_count.bit_length() - 1
    slots = jnp.arange(slot_count, dtype=jnp.int32)
    tok_rows, feat_dev = tokens.shape
    top_count = experts_of.shape[1]
    pairs = tok_rows * top_count
    capacity = 2 * pairs // slot_count
    cells = slot_count * capacity
    rows = cells // ring
    twins = hid_count // ring

    largest = jnp.max(jnp.bitwise_xor(partner, slots))
    bit_range = jnp.arange(levels, dtype=jnp.int32)
    chosen_bit = jnp.sum(
        jnp.where(largest == jnp.left_shift(jnp.int32(1), bit_range), bit_range, 0)
    )
    staying = jnp.sum(jnp.where(slots == own_slot, partner, 0)) == own_slot

    first_bits, second_bits, third_bits = range(1, 4), range(1), range(4, levels)

    def move(parts, arrived=None, bits=range(levels)):
        def branch(bit):
            if bit in bits:
                return lambda parts, arrived: [from_partner(part, bit) for part in parts]
            return lambda parts, arrived: arrived

        return lax.switch(
            chosen_bit, [branch(bit) for bit in range(levels)], parts, arrived or parts
        )

    stacked, experts_of, tokens, out_grad = lax.optimization_barrier(
        (jnp.stack([w_in, w_out]), experts_of, tokens, out_grad)
    )
    weights = lax.all_gather(
        stacked, "hid", axis=1, tiled=True, axis_index_groups=line_groups(hid_count)
    )

    chosen = experts_of.reshape(-1)
    onehot = (chosen[:, None] == slots[None, :]).astype(jnp.int32)
    rank = jnp.sum(jnp.cumsum(onehot, axis=0) * onehot, axis=1) - 1
    owner = jnp.sum(
        jnp.where(place_before[None, :] == slots[:, None], slots[None, :], 0), axis=1
    )
    target = jnp.sum(onehot * owner[None, :], axis=1)
    cell = target * capacity + rank
    pair_hit = cell[:, None] == jnp.arange(cells, dtype=jnp.int32)[None, :]
    gate_cell = jnp.sum(jnp.where(pair_hit, gates.reshape(-1)[:, None], 0.0), axis=0)
    picker = jnp.sum(
        pair_hit.astype(jnp.bfloat16).reshape(tok_rows, top_count, cells), axis=1
    )

    x_send = jnp.dot(picker.T, tokens, preferred_element_type=jnp.float32)
    grad_cell = jnp.dot(picker.T, out_grad, preferred_element_type=jnp.float32)
    dy_send = gate_cell[:, None] * grad_cell
    sent = jnp.concatenate(
        [
            part.astype(jnp.bfloat16).reshape(slot_count, capacity, feat_dev)
            for part in (x_send, dy_send)
        ],
        axis=1,
    )
    here = swap(sent, "expert")
    here = jnp.broadcast_to(
        here.reshape(1, ring, 2 * rows, feat_dev), (twins, ring, 2 * rows, feat_dev)
    ).reshape(hid_count, 2 * rows, feat_dev)
    here, w_in = lax.optimization_barrier((here, w_in))
    here = swap(here, "hid")
    w_moved = move([w_in], bits=first_bits)
    weights, w_in, w_moved = lax.optimization_barrier((weights, w_in, w_moved))
    wa_full, wb_full = weights[0], weights[1]
    w_moved = move([w_in], w_moved, bits=second_bits)
    here, w_moved = lax.optimization_barrier((here, w_moved))
    here = here.reshape(hid_count, slot_count // ring, 2, capacity, feat_dev)
    x_rows, dy_rows = [
        jnp.concatenate(
            [here[i, :, kind].reshape(rows, feat_dev) for i in range(hid_count)], axis=1
        )
        for kind in range(2)
    ]

    pre = lax.dot_general(
        x_rows, wa_full, (((1,), (1,)), ((), ())), preferred_element_type=jnp.float32
    )
    act = jax.nn.silu(pre).astype(jnp.bfloat16)
    sig = jax.nn.sigmoid(pre)
    dact = lax.dot_general(
        dy_rows, wb_full, (((1,), (1,)), ((), ())), preferred_element_type=jnp.float32
    )
    dpre = (dact * sig * (1.0 + pre * (1.0 - sig))).astype(jnp.bfloat16)

    y_part = jnp.dot(act, wb_full, preferred_element_type=jnp.float32).astype(jnp.bfloat16)
    dx_part = jnp.dot(dpre, wa_full, preferred_element_type=jnp.float32).astype(jnp.bfloat16)
    back = jnp.concatenate(
        [
            part.reshape(slot_count // ring, 1, capacity, hid_count * feat_dev)
            for part in (y_part, dx_part)
        ],
        axis=1,
    )
    back = jnp.transpose(back.reshape(2 * rows, hid_count, feat_dev), (1, 0, 2))
    back, dpre = lax.optimization_barrier((back, dpre))
    back = swap(back, "hid")
    grad_part = jnp.dot(dpre.T, x_rows, preferred_element_type=jnp.float32).astype(jnp.bfloat16)
    grads = lax.psum_scatter(
        grad_part,
        "hid",
        scatter_dimension=0,
        tiled=True,
        axis_index_groups=line_groups(hid_count),
    )
    grad_part, w_in, w_moved = lax.optimization_barrier((grad_part, w_in, w_moved))
    (w_moved,) = move([w_in], w_moved, bits=third_bits)
    back, _, w_moved = lax.optimization_barrier((back, grad_part, w_moved))
    back = jnp.sum(
        back.reshape(twins, slot_count, 2 * capacity, feat_dev).astype(jnp.float32), axis=0
    ).astype(jnp.bfloat16)

    back = swap(back, "expert")
    grads = grads.astype(jnp.float32)
    states = new_moments(m_in, v_in, grads)
    moved = move(states)
    back, states, moved = lax.optimization_barrier((back, states, moved))
    y_back, dx_back = back[:, :capacity], back[:, capacity:]
    y_wide = y_back.reshape(cells, feat_dev).astype(jnp.float32)
    gate_cell_grad = jnp.sum(grad_cell * y_wide, axis=1)
    gate_part = jnp.sum(jnp.where(pair_hit, gate_cell_grad[None, :], 0.0), axis=1)
    gate_part = gate_part.reshape(tok_rows, top_count).T
    gate_part = jnp.broadcast_to(gate_part[None], (hid_count, top_count, tok_rows))
    gate_grad = jnp.sum(swap(gate_part, "hid"), axis=0).T

    y_wide = gate_cell[:, None] * y_wide
    y_high = y_wide.astype(jnp.bfloat16)
    y_low = (y_wide - y_high.astype(jnp.float32)).astype(jnp.bfloat16)
    mixed = jnp.dot(
        jnp.concatenate([picker, picker], axis=1),
        jnp.concatenate([y_high, y_low], axis=0),
        preferred_element_type=jnp.float32,
    ).astype(jnp.bfloat16)
    input_grad = jnp.dot(
        picker, dx_back.reshape(cells, feat_dev), preferred_element_type=jnp.float32
    ).astype(jnp.bfloat16)

    states = [new_weight(w_in, *states)] + states
    moved = [new_weight(w_moved, *moved)] + moved
    new_w, new_m, new_v = [jnp.where(staying, own, other) for own, other in zip(states, moved)]
    return mixed, input_grad, gate_grad, new_w[None], new_m[None], new_v[None]


def solution(mesh):
    return jax.shard_map(
        on_device,
        mesh=mesh,
        in_specs=(
            P("expert", "hid"),
            P("expert", "hid"),
            P("expert", None),
            P("expert", None),
            P(),
            P(),
            P("expert", "hid", None),
            P("expert", "hid", None),
            P("expert", "hid", None),
            P("expert", "hid", None),
        ),
        out_specs=(
            P("expert", "hid"),
            P("expert", "hid"),
            P("expert", None),
            P("expert", "hid", None),
            P("expert", "hid", None),
            P("expert", "hid", None),
        ),
        check_vma=False,
    )
```
